32 devices in a mesh: sub: 32 (over z, y, x, core).
Axes of the slice: x: 2, y: 2, z: 4, core: 2. Of those that a mesh axis runs over, the one named last changes fastest.
Arguments:
- pool_inputs: bfloat16 [16384, 4096], P('sub'), may hold values from -6 to 6
- pool_targets: bfloat16 [16384, 4096], P('sub'), may hold values from -6 to 6
- row_picks: int32 [8, 8192], P(None, 'sub'), may hold values from 0 to 511
- weight_in: float32 [4096, 8192], P(None, 'sub'), may hold values from -6 to 6
- weight_out: float32 [4096, 8192], P(None, 'sub'), may hold values from -6 to 6
- eval_inputs: bfloat16 [64, 4096], P('sub'), may hold values from -6 to 6
- handover: int32 [1024], replicated, may hold values from 0 to 1023, as said below
Outputs:
- trained_in: float32 [4096, 8192], P(None, 'sub')
- trained_out: float32 [4096, 8192], P(None, 'sub')
- prediction: float32 [64, 4096], P('sub')
The draws below stay inside these ranges and needn't reach their ends.
Inputs may be any that keep to these rules, and one draw needn't show every extreme that they name: `row_picks`: indices into the subnet's own 512 resident rows. handover[g] is the new position of neuron group g (neurons 8 g to 8 g + 7); every position is taken once, and no two groups of one subnet move to the same subnet.
All inputs are finite; a program needn't handle non-finite values.
Results may differ from the reference program's by a relative error of at most 0.0065.
Values may be sent and summed in bfloat16 or wider, within the bound.
A program may use at most 192 MiB of HBM per device.

```python
import math
import jax
import jax.numpy as jnp
from jax import lax

D = 4096
HID_DEV = 256
GROUP = 8
STEPS = 4
BATCH = 256
POOL = 512
FF = 8192
GROUPS = 1024
POOLS = 16384
BATCHES = 8192
EVALS = 64


def unit_field(key, rows, columns):
    key_value = jax.random.fold_in(key, 0)
    return jax.random.truncated_normal(key_value, -6.0, 6.0, (rows, columns), jnp.float32)


def draw_pool_inputs(key, part):
    return unit_field(jax.random.fold_in(key, 11), POOLS, D).astype(jnp.bfloat16)


def draw_pool_targets(key, part):
    return unit_field(jax.random.fold_in(key, 12), POOLS, D).astype(jnp.bfloat16)


def draw_eval_inputs(key, part):
    return unit_field(jax.random.fold_in(key, 13), EVALS, D).astype(jnp.bfloat16)


def draw_weight_in(key, part):
    return unit_field(jax.random.fold_in(key, 14), D, FF).astype(jnp.float32)


def draw_weight_out(key, part):
    return unit_field(jax.random.fold_in(key, 15), D, FF).astype(jnp.float32)


def draw_handover(key, part):
    group_count = HID_DEV // GROUP
    owners = GROUPS // group_count
    key_relabel, key_shift, key_offset, key_source, key_slot = jax.random.split(key, 5)
    relabel = jax.random.permutation(key_relabel, owners).astype(jnp.int32)
    shifted = jax.random.permutation(key_shift, owners).astype(jnp.int32)
    offset_pick = jax.random.permutation(key_offset, owners).astype(jnp.int32)[:group_count]
    lane_index = jax.vmap(lambda one_key: jax.random.permutation(one_key, group_count))(jax.random.split(key_source, owners)).astype(jnp.int32)
    slot_order = jax.vmap(lambda one_key: jax.random.permutation(one_key, group_count))(jax.random.split(key_slot, owners)).astype(jnp.int32)
    destination = relabel[(shifted[:, None] + offset_pick[lane_index]) % owners]
    slot_index = slot_order[destination, lane_index]
    return (destination * group_count + slot_index).reshape(-1).astype(jnp.int32)


def plant(drawn, own_key, least, largest):
    place = [jax.random.randint(jax.random.fold_in(own_key, axis), (), 0, length) for axis, length in enumerate(drawn.shape)]
    main_axis = drawn.shape.index(max(drawn.shape))
    beside = place[:main_axis] + [(place[main_axis] + 1) % drawn.shape[main_axis]] + place[main_axis + 1:]
    return drawn.at[tuple(place)].set(least).at[tuple(beside)].set(largest)


def setup_inputs(seed: int = 0) -> dict:
    key_of = jax.random.split(jax.random.key(seed), 8)
    pool_inputs = draw_pool_inputs(jax.random.fold_in(key_of[7], 71), 0)
    pool_targets = draw_pool_targets(jax.random.fold_in(key_of[7], 71), 0)
    row_picks = plant(jax.random.randint(key_of[2], (2 * STEPS, BATCHES), 0, POOL), jax.random.fold_in(key_of[2], 1), 0, POOL - 1).astype(jnp.int32)
    weight_in = draw_weight_in(jax.random.fold_in(key_of[7], 71), 0)
    weight_out = draw_weight_out(jax.random.fold_in(key_of[7], 71), 0)
    eval_inputs = draw_eval_inputs(jax.random.fold_in(key_of[7], 71), 0)
    handover = draw_handover(jax.random.fold_in(key_of[7], 71), 0)
    return {"pool_inputs": pool_inputs, "pool_targets": pool_targets, "row_picks": row_picks, "weight_in": weight_in, "weight_out": weight_out, "eval_inputs": eval_inputs, "handover": handover}


tanh_coef = 0.7978845608028654
cubic_coef = 0.044715
step_rate = 0.5

def gelu_value(inputs):
    inner_term = tanh_coef * (inputs + cubic_coef * inputs * inputs * inputs)
    return 0.5 * inputs * (1.0 + jnp.tanh(inner_term))

def gelu_parts(inputs):
    tanh_part = jnp.tanh(tanh_coef * (inputs + cubic_coef * inputs * inputs * inputs))
    values = 0.5 * inputs * (1.0 + tanh_part)
    slopes = 0.5 * (1.0 + tanh_part) + 0.5 * inputs * (1.0 - tanh_part * tanh_part) * tanh_coef * (1.0 + 3.0 * cubic_coef * inputs * inputs)
    return (values, slopes)

def train_step(layer_in, layer_out, batch_rows, batch_goals, scale_in, scale_out):
    in_half = layer_in.astype(jnp.bfloat16)
    out_half = layer_out.astype(jnp.bfloat16)
    before = jnp.dot(batch_rows, in_half, preferred_element_type=jnp.float32) * scale_in
    values, slopes = gelu_parts(before)
    activity = values.astype(jnp.bfloat16)
    branch = jnp.dot(activity, out_half.T, preferred_element_type=jnp.float32) * scale_out
    errors = (branch - batch_goals.astype(jnp.float32)).astype(jnp.bfloat16)
    grad_out = jnp.dot(errors.T, activity, preferred_element_type=jnp.float32) * scale_out
    backward = (jnp.dot(errors, out_half, preferred_element_type=jnp.float32) * scale_out * slopes).astype(jnp.bfloat16)
    grad_in = jnp.dot(batch_rows.T, backward, preferred_element_type=jnp.float32) * scale_in
    return (layer_in - step_rate * grad_in, layer_out - step_rate * grad_out)

def run_round(weight_in, weight_out, pool_inputs, pool_targets, row_picks, first_turn):
    owners = FF // HID_DEV
    scale_in = 1.0 / math.sqrt(D)
    scale_out = 1.0 / math.sqrt(FF)
    blocks_in = weight_in.reshape(D, owners, HID_DEV).transpose(1, 0, 2)
    blocks_out = weight_out.reshape(D, owners, HID_DEV).transpose(1, 0, 2)
    inputs_split = pool_inputs.reshape(owners, POOL, D)
    targets_split = pool_targets.reshape(owners, POOL, D)
    picks_split = row_picks[first_turn:first_turn + STEPS].reshape(STEPS, owners, BATCH).transpose(1, 0, 2)

    def subnet(packed):
        layer_in, layer_out, rows_pool, goals_pool, chosen = packed
        for turn_index in range(STEPS):
            batch_rows = jnp.take(rows_pool, chosen[turn_index], axis=0)
            batch_goals = jnp.take(goals_pool, chosen[turn_index], axis=0)
            layer_in, layer_out = train_step(layer_in, layer_out, batch_rows, batch_goals, scale_in, scale_out)
        return (layer_in, layer_out)
    new_in, new_out = lax.map(subnet, (blocks_in, blocks_out, inputs_split, targets_split, picks_split))
    return (new_in.transpose(1, 0, 2).reshape(D, FF), new_out.transpose(1, 0, 2).reshape(D, FF))

def reference(pool_inputs, pool_targets, row_picks, weight_in, weight_out, eval_inputs, handover):
    scale_in = 1.0 / math.sqrt(D)
    scale_out = 1.0 / math.sqrt(FF)
    middle_in, middle_out = run_round(weight_in, weight_out, pool_inputs, pool_targets, row_picks, 0)
    eval_act = gelu_value(jnp.dot(eval_inputs, middle_in.astype(jnp.bfloat16), preferred_element_type=jnp.float32) * scale_in).astype(jnp.bfloat16)
    prediction = jnp.dot(eval_act, middle_out.astype(jnp.bfloat16).T, preferred_element_type=jnp.float32) * scale_out
    inverse = jnp.zeros((GROUPS,), jnp.int32).at[handover].set(jnp.arange(GROUPS, dtype=jnp.int32))
    columns = (inverse[:, None] * GROUP + jnp.arange(GROUP, dtype=jnp.int32)[None, :]).reshape(-1)
    handed_in = jnp.take(middle_in, columns, axis=1)
    handed_out = jnp.take(middle_out, columns, axis=1)
    trained_in, trained_out = run_round(handed_in, handed_out, pool_inputs, pool_targets, row_picks, STEPS)
    return (trained_in, trained_out, prediction)
```

```python
import functools
import math

import jax
import jax.numpy as jnp
from jax import lax
from jax.experimental import pallas as pl
from jax.experimental.pallas import tpu as pltpu
from jax.sharding import PartitionSpec as P

GROUP = 8
STEPS = 4
CHUNK = 1024
VMEM_LIMIT = 58 * 1024 * 1024
MESH_IDS = pl.DeviceIdType.MESH

tanh_coef = 0.7978845608028654
cubic_coef = 0.044715
step_rate = 0.5
F32 = jnp.float32
BF16 = jnp.bfloat16


def gelu_value(inputs):
    inner_term = tanh_coef * (inputs + cubic_coef * inputs * inputs * inputs)
    return 0.5 * inputs * (1.0 + jnp.tanh(inner_term))


def gelu_parts(inputs):
    tanh_part = jnp.tanh(tanh_coef * (inputs + cubic_coef * inputs * inputs * inputs))
    values = 0.5 * inputs * (1.0 + tanh_part)
    slopes = 0.5 * (1.0 + tanh_part) + 0.5 * inputs * (1.0 - tanh_part * tanh_part) * tanh_coef * (
        1.0 + 3.0 * cubic_coef * inputs * inputs
    )
    return (values, slopes)


def dot_nn(left, right):
    return jnp.dot(left, right, preferred_element_type=F32)


def dot_nt(left, right):
    return lax.dot_general(left, right, (((1,), (1,)), ((), ())), preferred_element_type=F32)


def chunks_of(width):
    return [pl.ds(first, CHUNK) for first in range(0, width, CHUNK)]


def one_hot(picks, pool):
    places = lax.broadcasted_iota(jnp.int32, (picks.shape[0], pool), 1)
    return jnp.where(places == picks, 1.0, 0.0).astype(BF16)


def train_step(in_t, out_t, rows_at, goals_at, scale_in, scale_out):
    width = in_t.shape[1]
    before = None
    for part in chunks_of(width):
        term = dot_nt(rows_at(part, True), in_t[:, part].astype(BF16))
        before = term if before is None else before + term
    values, slopes = gelu_parts(before * scale_in)
    activity = values.astype(BF16)
    activity_t = values.T.astype(BF16)
    back = None
    for part in chunks_of(width):
        master = out_t[:, part]
        half = master.astype(BF16)
        errors = (dot_nn(activity, half) * scale_out - goals_at(part)).astype(BF16)
        term = dot_nt(errors, half)
        back = term if back is None else back + term
        out_t[:, part] = master - dot_nn(activity_t, errors) * (step_rate * scale_out)
    backward_t = (back * scale_out * slopes).T.astype(BF16)
    for part in chunks_of(width):
        in_t[:, part] = in_t[:, part] - dot_nn(backward_t, rows_at(part, False)) * (
            step_rate * scale_in
        )


def first_round(
    scale_in, scale_out, chosen, picks, pool_in, pool_out, weight_in, weight_out, send, in_t, out_t, rows
):
    width, pool = weight_in.shape[0], pool_in.shape[0]
    for part in chunks_of(width):
        in_t[:, part] = weight_in[part, :].T
        out_t[:, part] = weight_out[part, :].T

    @pl.loop(0, STEPS)
    def _(turn):
        select = one_hot(picks[turn], pool)

        def rows_at(part, fresh):
            if fresh:
                rows[:, part] = dot_nn(select, pool_in[:, part]).astype(BF16)
            return rows[:, part]

        def goals_at(part):
            return dot_nn(select, pool_out[:, part])

        train_step(in_t, out_t, rows_at, goals_at, scale_in, scale_out)

    @pl.loop(0, send.shape[0])
    def _(owner):
        place = pl.ds(pl.multiple_of(chosen[owner] * GROUP, GROUP), GROUP)
        send[owner] = jnp.concatenate([in_t[place, :], out_t[place, :]], axis=0).astype(BF16)


def hand_over(
    owners, scale_in, scale_out,
    send, picks, pool_in, pool_out, evals, valid,
    landed, rows_out, goals_out, prediction,
    sent, inputs, targets, rows, goals, partial, share, arrived,
    send_sem, recv_sem, share_send, share_recv, local_sem, out_sem,
):
    me = lax.axis_index("sub")
    barrier = pltpu.get_barrier_semaphore()

    def other(turn):
        return lax.rem(me + turn, owners)

    def source(turn):
        return lax.rem(me - turn + owners, owners)

    @pl.loop(1, owners)
    def _(turn):
        pl.semaphore_signal(barrier, inc=1, device_id=(other(turn),), device_id_type=MESH_IDS)

    sent_copy = pltpu.make_async_copy(send, sent, local_sem.at[0])
    own_copy = pltpu.make_async_copy(send.at[me], landed.at[me], local_sem.at[1])
    inputs_copy = pltpu.make_async_copy(pool_in, inputs, local_sem.at[2])
    targets_copy = pltpu.make_async_copy(pool_out, targets, local_sem.at[3])
    sent_copy.start()
    own_copy.start()
    inputs_copy.start()
    targets_copy.start()
    pl.semaphore_wait(barrier, owners - 1)

    def moving(peer, slot):
        return pltpu.make_async_remote_copy(
            src_ref=send.at[peer], dst_ref=landed.at[me],
            send_sem=send_sem.at[peer], recv_sem=recv_sem.at[slot],
            device_id=(peer,), device_id_type=MESH_IDS,
        )

    def sharing(peer, slot):
        return pltpu.make_async_remote_copy(
            src_ref=share.at[peer], dst_ref=arrived.at[me],
            send_sem=share_send.at[peer], recv_sem=share_recv.at[slot],
            device_id=(peer,), device_id_type=MESH_IDS,
        )

    @pl.loop(1, owners)
    def _(turn):
        moving(other(turn), me).start()

    sent_copy.wait()
    slots = owners * 2 * GROUP
    width = sent.shape[2]
    before = dot_nt(evals[...], sent[...].reshape(slots, width)) * scale_in
    acts = pltpu.roll(gelu_value(before), GROUP, 1) * valid[...]
    acts = acts.astype(BF16)
    for part in chunks_of(width):
        partial[:, part] = dot_nn(acts, sent[:, :, part].reshape(slots, CHUNK)) * scale_out
    per_owner = partial.shape[0] // owners
    pieces, piece = 16 // per_owner, width * per_owner // 16

    @pl.loop(0, partial.shape[0] // 8)
    def _(block):
        tile = partial[pl.ds(pl.multiple_of(block * 8, 8), 8), :]
        for peer in range(8 // per_owner):
            mine = tile[peer * per_owner : (peer + 1) * per_owner]
            share[block * (8 // per_owner) + peer] = jnp.concatenate(
                [mine[:, k * piece : (k + 1) * piece] for k in range(pieces)], axis=0
            ).astype(BF16)

    @pl.loop(1, owners)
    def _(turn):
        sharing(other(turn), me).start()

    inputs_copy.wait()
    targets_copy.wait()
    pool = inputs.shape[0]

    @pl.loop(0, STEPS)
    def _(turn):
        select = one_hot(picks[turn], pool)
        for part in chunks_of(width):
            rows[turn, :, part] = dot_nn(select, inputs[:, part]).astype(BF16)
            goals[turn, :, part] = dot_nn(select, targets[:, part]).astype(BF16)

    rows_copy = pltpu.make_async_copy(rows, rows_out, out_sem.at[0])
    goals_copy = pltpu.make_async_copy(goals, goals_out, out_sem.at[1])
    rows_copy.start()
    goals_copy.start()
    rows_copy.wait()
    goals_copy.wait()
    own_copy.wait()

    @pl.loop(1, owners)
    def _(turn):
        moving(other(turn), me).wait_send()
        moving(other(turn), source(turn)).wait_recv()

    @pl.loop(1, owners)
    def _(turn):
        sharing(other(turn), me).wait_send()
        sharing(other(turn), source(turn)).wait_recv()

    prediction[...] = share[me].astype(F32)

    @pl.loop(1, owners)
    def _(turn):
        prediction[...] += arrived[source(turn)].astype(F32)


def second_round(
    scale_in, scale_out, sources, landed, rows_in, goals_in, trained_in, trained_out,
    handed, in_t, out_t, rows, goals, handed_sem, rows_sem, goals_sem,
):
    groups = handed.shape[0]

    def fetch(slot):
        return pltpu.make_async_copy(landed.at[sources[slot]], handed.at[slot], handed_sem.at[slot])

    def rows_copy(turn):
        return pltpu.make_async_copy(rows_in.at[turn], rows.at[turn], rows_sem.at[turn])

    def goals_copy(turn):
        return pltpu.make_async_copy(goals_in.at[turn], goals.at[turn], goals_sem.at[turn])

    @pl.loop(0, groups)
    def _(slot):
        fetch(slot).start()

    @pl.loop(0, STEPS)
    def _(turn):
        rows_copy(turn).start()
        goals_copy(turn).start()

    @pl.loop(0, groups)
    def _(slot):
        fetch(slot).wait()
        slab = handed[slot].astype(F32)
        place = pl.ds(pl.multiple_of(slot * GROUP, GROUP), GROUP)
        in_t[place, :] = slab[:GROUP]
        out_t[place, :] = slab[GROUP:]

    @pl.loop(0, STEPS)
    def _(turn):
        rows_copy(turn).wait()
        goals_copy(turn).wait()
        train_step(
            in_t, out_t,
            lambda part, fresh: rows[turn, :, part],
            lambda part: goals[turn, :, part].astype(F32),
            scale_in, scale_out,
        )

    for part in chunks_of(in_t.shape[1]):
        trained_in[part, :] = in_t[:, part].T
        trained_out[part, :] = out_t[:, part].T


def per_device(pool_inputs, pool_targets, row_picks, weight_in, weight_out, eval_inputs, handover):
    owners = lax.axis_size("sub")
    my_index = lax.axis_index("sub")
    width, hidden = weight_in.shape
    pool = pool_inputs.shape[0]
    batch = row_picks.shape[1]
    per_owner = eval_inputs.shape[0]
    groups = hidden // GROUP
    total_groups = groups * owners
    scale_in = 1.0 / math.sqrt(width)
    scale_out = 1.0 / math.sqrt(hidden * owners)
    vmem = pl.BlockSpec(memory_space=pltpu.VMEM)
    smem = pl.BlockSpec(memory_space=pltpu.SMEM)
    anywhere = pl.BlockSpec(memory_space=pl.ANY)
    slab = (owners, 2 * GROUP, width)

    evals = lax.all_gather(eval_inputs, "sub", axis=0, tiled=True)
    picks = row_picks[:, :, None]

    targets = lax.dynamic_slice_in_dim(handover, my_index * groups, groups, 0) // groups
    matches = targets[None, :] == jnp.arange(owners, dtype=jnp.int32)[:, None]
    chosen = jnp.sum(jnp.where(matches, jnp.arange(groups, dtype=jnp.int32)[None, :], 0), axis=1)
    has_group = jnp.any(matches, axis=1)
    valid = jnp.where(
        has_group[:, None] & (jnp.arange(2 * GROUP) >= GROUP)[None, :], 1.0, 0.0
    ).reshape(1, -1)
    places = my_index * groups + jnp.arange(groups, dtype=jnp.int32)
    arriving = jnp.sum(
        jnp.where(
            handover[None, :] == places[:, None],
            jnp.arange(total_groups, dtype=jnp.int32)[None, :],
            0,
        ),
        axis=1,
    )
    sources = arriving // groups

    send = pl.pallas_call(
        functools.partial(first_round, scale_in, scale_out),
        out_shape=jax.ShapeDtypeStruct(slab, BF16),
        in_specs=[smem] + [vmem] * 5,
        out_specs=vmem,
        scratch_shapes=[
            pltpu.VMEM((hidden, width), F32),
            pltpu.VMEM((hidden, width), F32),
            pltpu.VMEM((batch, width), BF16),
        ],
        compiler_params=pltpu.CompilerParams(vmem_limit_bytes=VMEM_LIMIT),
        cost_estimate=pl.CostEstimate(
            flops=STEPS * 18 * batch * width * hidden, bytes_accessed=20 << 20, transcendentals=0
        ),
        name="first_round",
    )(chosen, picks[:STEPS], pool_inputs, pool_targets, weight_in, weight_out)

    rows_shape = (STEPS, batch, width)
    landed, rows, goals, prediction = pl.pallas_call(
        functools.partial(hand_over, owners, scale_in, scale_out),
        out_shape=[
            jax.ShapeDtypeStruct(slab, BF16),
            jax.ShapeDtypeStruct(rows_shape, BF16),
            jax.ShapeDtypeStruct(rows_shape, BF16),
            jax.ShapeDtypeStruct((16, per_owner * width // 16), F32),
        ],
        in_specs=[anywhere, vmem, anywhere, anywhere, vmem, vmem],
        out_specs=[anywhere, anywhere, anywhere, vmem],
        scratch_shapes=[
            pltpu.VMEM(slab, BF16),
            pltpu.VMEM((pool, width), BF16),
            pltpu.VMEM((pool, width), BF16),
            pltpu.VMEM(rows_shape, BF16),
            pltpu.VMEM(rows_shape, BF16),
            pltpu.VMEM((per_owner * owners, width), F32),
            pltpu.VMEM((owners, 16, per_owner * width // 16), BF16),
            pltpu.VMEM((owners, 16, per_owner * width // 16), BF16),
            pltpu.SemaphoreType.DMA((owners,)),
            pltpu.SemaphoreType.DMA((owners,)),
            pltpu.SemaphoreType.DMA((owners,)),
            pltpu.SemaphoreType.DMA((owners,)),
            pltpu.SemaphoreType.DMA((4,)),
            pltpu.SemaphoreType.DMA((2,)),
        ],
        compiler_params=pltpu.CompilerParams(
            vmem_limit_bytes=VMEM_LIMIT, collective_id=0, has_side_effects=True
        ),
        cost_estimate=pl.CostEstimate(
            flops=STEPS * 8 * batch * width * hidden, bytes_accessed=40 << 20, transcendentals=0
        ),
        name="hand_over",
    )(send, picks[STEPS:], pool_inputs, pool_targets, evals, valid)

    trained_in, trained_out = pl.pallas_call(
        functools.partial(second_round, scale_in, scale_out),
        out_shape=[jax.ShapeDtypeStruct((width, hidden), F32)] * 2,
        in_specs=[smem, anywhere, anywhere, anywhere],
        out_specs=[vmem, vmem],
        scratch_shapes=[
            pltpu.VMEM((groups, 2 * GROUP, width), BF16),
            pltpu.VMEM((hidden, width), F32),
            pltpu.VMEM((hidden, width), F32),
            pltpu.VMEM(rows_shape, BF16),
            pltpu.VMEM(rows_shape, BF16),
            pltpu.SemaphoreType.DMA((groups,)),
            pltpu.SemaphoreType.DMA((STEPS,)),
            pltpu.SemaphoreType.DMA((STEPS,)),
        ],
        compiler_params=pltpu.CompilerParams(vmem_limit_bytes=VMEM_LIMIT),
        cost_estimate=pl.CostEstimate(
            flops=STEPS * 10 * batch * width * hidden, bytes_accessed=28 << 20, transcendentals=0
        ),
        name="second_round",
    )(sources, landed, rows, goals)

    pieces = 16 // per_owner
    prediction = (
        prediction.reshape(pieces, per_owner, width // pieces)
        .transpose(1, 0, 2)
        .reshape(per_owner, width)
    )
    return (trained_in, trained_out, prediction)


def solution(mesh):
    in_specs = (
        P("sub", None),
        P("sub", None),
        P(None, "sub"),
        P(None, "sub"),
        P(None, "sub"),
        P("sub", None),
        P(),
    )
    out_specs = (P(None, "sub"), P(None, "sub"), P("sub", None))
    return jax.shard_map(
        per_device, mesh=mesh, in_specs=in_specs, out_specs=out_specs, check_vma=False
    )
```

```python
import functools
import math

import jax
import jax.numpy as jnp
from jax import lax
from jax.experimental import pallas as pl
from jax.experimental.pallas import tpu as pltpu
from jax.sharding import PartitionSpec as P

GROUP = 8
STEPS = 4
CHUNK = 1024
VMEM_LIMIT = 58 * 1024 * 1024
MESH_IDS = pl.DeviceIdType.MESH

tanh_coef = 0.7978845608028654
cubic_coef = 0.044715
step_rate = 0.5
F32 = jnp.float32
BF16 = jnp.bfloat16


def gelu_value(inputs):
    inner_term = tanh_coef * (inputs + cubic_coef * inputs * inputs * inputs)
    return 0.5 * inputs * (1.0 + jnp.tanh(inner_term))


def gelu_parts(inputs):
    tanh_part = jnp.tanh(tanh_coef * (inputs + cubic_coef * inputs * inputs * inputs))
    values = 0.5 * inputs * (1.0 + tanh_part)
    slopes = 0.5 * (1.0 + tanh_part) + 0.5 * inputs * (1.0 - tanh_part * tanh_part) * tanh_coef * (
        1.0 + 3.0 * cubic_coef * inputs * inputs
    )
    return (values, slopes)


def dot_nn(left, right):
    return jnp.dot(left, right, preferred_element_type=F32)


def dot_nt(left, right):
    return lax.dot_general(left, right, (((1,), (1,)), ((), ())), preferred_element_type=F32)


def chunks_of(width):
    return [pl.ds(first, CHUNK) for first in range(0, width, CHUNK)]


def one_hot(picks_t, turn, pool):
    turns = lax.broadcasted_iota(jnp.int32, picks_t.shape, 1)
    picks = jnp.sum(jnp.where(turns == turn, picks_t, 0.0), axis=1, keepdims=True)
    places = lax.broadcasted_iota(jnp.int32, (picks.shape[0], pool), 1).astype(F32)
    return jnp.where(places == picks, 1.0, 0.0).astype(BF16)


def train_step(in_t, out_t, rows_at, goals_at, scale_in, scale_out):
    width = in_t.shape[1]
    before = None
    for part in chunks_of(width):
        term = dot_nt(rows_at(part, True), in_t[:, part].astype(BF16))
        before = term if before is None else before + term
    values, slopes = gelu_parts(before * scale_in)
    activity = values.astype(BF16)
    activity_t = values.T.astype(BF16)
    back = None
    for part in chunks_of(width):
        master = out_t[:, part]
        half = master.astype(BF16)
        errors = (dot_nn(activity, half) * scale_out - goals_at(part)).astype(BF16)
        term = dot_nt(errors, half)
        back = term if back is None else back + term
        out_t[:, part] = master - dot_nn(activity_t, errors) * (step_rate * scale_out)
    backward_t = (back * scale_out * slopes).T.astype(BF16)
    for part in chunks_of(width):
        in_t[:, part] = in_t[:, part] - dot_nn(backward_t, rows_at(part, False)) * (
            step_rate * scale_in
        )


def first_round(
    scale_in, scale_out,
    chosen, picks, pool_in, pool_out, weight_in, weight_out,
    send,
    inputs, targets, start_in, start_out, in_t, out_t, rows, load_sem,
):
    width, pool = weight_in.shape[0], pool_in.shape[0]
    loads = [
        pltpu.make_async_copy(source, target, load_sem.at[k])
        for k, (source, target) in enumerate(
            [(weight_in, start_in), (weight_out, start_out), (pool_in, inputs), (pool_out, targets)]
        )
    ]
    for load in loads:
        load.start()
    picks_t = picks[...].astype(F32).T
    loads[0].wait()
    for part in chunks_of(width):
        in_t[:, part] = start_in[part, :].T
    loads[1].wait()
    for part in chunks_of(width):
        out_t[:, part] = start_out[part, :].T
    loads[2].wait()
    loads[3].wait()

    @pl.loop(0, STEPS)
    def _(turn):
        select = one_hot(picks_t, turn, pool)

        def rows_at(part, fresh):
            if fresh:
                rows[:, part] = dot_nn(select, inputs[:, part]).astype(BF16)
            return rows[:, part]

        def goals_at(part):
            return dot_nn(select, targets[:, part])

        train_step(in_t, out_t, rows_at, goals_at, scale_in, scale_out)

    @pl.loop(0, send.shape[0])
    def _(owner):
        place = pl.ds(pl.multiple_of(chosen[owner] * GROUP, GROUP), GROUP)
        send[owner] = jnp.concatenate([in_t[place, :], out_t[place, :]], axis=0).astype(BF16)


def hand_over(
    owners, scale_in, scale_out,
    send, picks, pool_in, pool_out, my_evals, valid,
    landed, rows_out, goals_out, prediction,
    sent, inputs, targets, rows, goals, all_evals, gathered,
    send_sem, recv_sem, eval_send, eval_recv, share_send, share_recv, local_sem, out_sem,
    *sums,
):
    me = lax.axis_index("sub")
    bits = owners.bit_length() - 1
    kept, added = sums[:bits], sums[bits:]
    barrier = pltpu.get_barrier_semaphore()

    def other(turn):
        return lax.rem(me + turn, owners)

    @pl.loop(1, owners)
    def _(turn):
        pl.semaphore_signal(barrier, inc=1, device_id=(other(turn),), device_id_type=MESH_IDS)

    sent_copy = pltpu.make_async_copy(send, sent, local_sem.at[0])
    own_copy = pltpu.make_async_copy(send.at[me], landed.at[me], local_sem.at[1])
    inputs_copy = pltpu.make_async_copy(pool_in, inputs, local_sem.at[2])
    targets_copy = pltpu.make_async_copy(pool_out, targets, local_sem.at[3])
    sent_copy.start()
    own_copy.start()
    inputs_copy.start()
    targets_copy.start()
    gathered[me] = my_evals[...]
    pl.semaphore_wait(barrier, owners - 1)

    def spreading(peer, slot):
        return pltpu.make_async_remote_copy(
            src_ref=my_evals, dst_ref=gathered.at[me],
            send_sem=eval_send.at[peer], recv_sem=eval_recv.at[slot],
            device_id=(peer,), device_id_type=MESH_IDS,
        )

    def moving(peer, slot):
        return pltpu.make_async_remote_copy(
            src_ref=send.at[peer], dst_ref=landed.at[me],
            send_sem=send_sem.at[peer], recv_sem=recv_sem.at[slot],
            device_id=(peer,), device_id_type=MESH_IDS,
        )

    def summing(bit):
        mine = lax.rem(me // (1 << bit), 2)
        peer = me + (1 - 2 * mine) * (1 << bit)
        return mine, pltpu.make_async_remote_copy(
            src_ref=kept[bit].at[:, 1 - mine], dst_ref=added[bit],
            send_sem=share_send.at[bit], recv_sem=share_recv.at[bit],
            device_id=(peer,), device_id_type=MESH_IDS,
        )

    @pl.loop(1, owners)
    def _(turn):
        spreading(other(turn), me).start()

    quarter = owners // 4
    high, low = me // quarter, lax.rem(me, quarter)

    def move_some(first, last):
        @pl.loop(first, last)
        def _(step):
            low_peer = lax.rem(low + step + 1, quarter)
            for hop in (2, 1, 3):
                peer = lax.rem(high + hop, 4) * quarter + low_peer
                moving(peer, me).start()

            @pl.when(step < quarter - 1)
            def _():
                moving(high * quarter + low_peer, me).start()

    cuts = [quarter * (k + 1) // (bits + 1) for k in range(bits)] + [quarter]
    cuts[0] = max(cuts[0], 2)
    cuts = [0] + [max(cuts[0], cut) for cut in cuts]
    move_some(cuts[0], cuts[1])

    sent_copy.wait()
    per_owner = all_evals.shape[0] // owners
    slots = owners * 2 * GROUP
    width = sent.shape[2]
    pieces, piece = 16 // per_owner, width * per_owner // 16
    together = 8 // per_owner

    @pl.loop(1, owners)
    def _(turn):
        spreading(other(turn), me).wait_send()
        spreading(other(turn), other(turn)).wait_recv()

    @pl.loop(0, owners // together)
    def _(block):
        slabs = [gathered[block * together + k].astype(F32) for k in range(together)]
        for k in range(pieces):
            all_evals[pl.ds(pl.multiple_of(block * 8, 8), 8), pl.ds(k * piece, piece)] = (
                jnp.concatenate([slab[k * per_owner : (k + 1) * per_owner] for slab in slabs], axis=0)
            )

    before = dot_nt(all_evals[...].astype(BF16), sent[...].reshape(slots, width)) * scale_in
    acts = (pltpu.roll(gelu_value(before), GROUP, 1) * valid[...]).astype(BF16)
    partial = all_evals
    for part in chunks_of(width):
        partial[:, part] = dot_nn(acts, sent[:, :, part].reshape(slots, CHUNK)) * scale_out

    @pl.loop(0, owners // together)
    def _(block):
        tile = partial[pl.ds(pl.multiple_of(block * 8, 8), 8), :]
        for k in range(together):
            mine = tile[k * per_owner : (k + 1) * per_owner]
            kept[0][block * (together // 2) + k // 2, k % 2] = jnp.concatenate(
                [mine[:, j * piece : (j + 1) * piece] for j in range(pieces)], axis=0
            ).astype(BF16)

    inputs_copy.wait()
    targets_copy.wait()
    pool = inputs.shape[0]
    picks_t = picks[...].astype(F32).T

    for bit in range(bits):
        mine, share = summing(bit)
        share.start()
        move_some(cuts[bit + 1], cuts[bit + 2])
        if bit < STEPS:
            select = one_hot(picks_t, STEPS + bit, pool)

            @pl.loop(0, width // CHUNK)
            def _(k):
                part = pl.ds(pl.multiple_of(k * CHUNK, CHUNK), CHUNK)
                rows[bit, :, part] = dot_nn(select, inputs[:, part]).astype(BF16)
                goals[bit, :, part] = dot_nn(select, targets[:, part]).astype(BF16)

        if bit == STEPS - 1:
            pltpu.make_async_copy(rows, rows_out, out_sem.at[0]).start()
            pltpu.make_async_copy(goals, goals_out, out_sem.at[1]).start()
        share.wait()
        if bit < bits - 1:
            @pl.loop(0, owners >> (bit + 2))
            def _(pair):
                for k in range(2):
                    slot = 2 * pair + k
                    kept[bit + 1][pair, k] = (
                        kept[bit][slot, mine].astype(F32) + added[bit][slot].astype(F32)
                    ).astype(BF16)
        else:
            prediction[...] = kept[bit][0, mine].astype(F32) + added[bit][0].astype(F32)

    pltpu.make_async_copy(rows, rows_out, out_sem.at[0]).wait()
    pltpu.make_async_copy(goals, goals_out, out_sem.at[1]).wait()
    own_copy.wait()

    @pl.loop(1, owners)
    def _(turn):
        moving(other(turn), me).wait_send()
        moving(other(turn), other(turn)).wait_recv()


def second_round(
    scale_in, scale_out, sources, landed, rows_in, goals_in, trained_in, trained_out,
    handed, in_t, out_t, rows, goals, done_in, done_out, handed_sem, rows_sem, goals_sem, done_sem,
):
    groups = handed.shape[0]

    def fetch(slot):
        return pltpu.make_async_copy(landed.at[sources[slot]], handed.at[slot], handed_sem.at[slot])

    def rows_copy(turn):
        return pltpu.make_async_copy(rows_in.at[turn], rows.at[turn], rows_sem.at[turn])

    def goals_copy(turn):
        return pltpu.make_async_copy(goals_in.at[turn], goals.at[turn], goals_sem.at[turn])

    @pl.loop(0, groups)
    def _(slot):
        fetch(slot).start()

    @pl.loop(0, STEPS)
    def _(turn):
        rows_copy(turn).start()
        goals_copy(turn).start()

    @pl.loop(0, groups)
    def _(slot):
        fetch(slot).wait()
        slab = handed[slot].astype(F32)
        place = pl.ds(pl.multiple_of(slot * GROUP, GROUP), GROUP)
        in_t[place, :] = slab[:GROUP]
        out_t[place, :] = slab[GROUP:]

    @pl.loop(0, STEPS)
    def _(turn):
        rows_copy(turn).wait()
        goals_copy(turn).wait()
        train_step(
            in_t, out_t,
            lambda part, fresh: rows[turn, :, part],
            lambda part: goals[turn, :, part].astype(F32),
            scale_in, scale_out,
        )

    stores = []
    for k, part in enumerate(chunks_of(in_t.shape[1])):
        for side, (master, done, trained) in enumerate(
            [(in_t, done_in, trained_in), (out_t, done_out, trained_out)]
        ):
            done[part, :] = master[:, part].T
            stores.append(
                pltpu.make_async_copy(done.at[part, :], trained.at[part, :], done_sem.at[2 * k + side])
            )
            stores[-1].start()
    for store in stores:
        store.wait()


def per_device(pool_inputs, pool_targets, row_picks, weight_in, weight_out, eval_inputs, handover):
    owners = lax.axis_size("sub")
    my_index = lax.axis_index("sub")
    width, hidden = weight_in.shape
    pool = pool_inputs.shape[0]
    batch = row_picks.shape[1]
    per_owner = eval_inputs.shape[0]
    groups = hidden // GROUP
    total_groups = groups * owners
    scale_in = 1.0 / math.sqrt(width)
    scale_out = 1.0 / math.sqrt(hidden * owners)
    vmem = pl.BlockSpec(memory_space=pltpu.VMEM)
    smem = pl.BlockSpec(memory_space=pltpu.SMEM)
    anywhere = pl.BlockSpec(memory_space=pl.ANY)
    slab = (owners, 2 * GROUP, width)
    bits = owners.bit_length() - 1

    pieces = 16 // per_owner
    piece = width // pieces
    evals = eval_inputs.reshape(per_owner, pieces, piece).transpose(1, 0, 2).reshape(16, piece)

    targets = lax.dynamic_slice_in_dim(handover, my_index * groups, groups, 0) // groups
    matches = targets[None, :] == jnp.arange(owners, dtype=jnp.int32)[:, None]
    chosen = jnp.sum(jnp.where(matches, jnp.arange(groups, dtype=jnp.int32)[None, :], 0), axis=1)
    has_group = jnp.any(matches, axis=1)
    valid = jnp.where(
        has_group[:, None] & (jnp.arange(2 * GROUP) >= GROUP)[None, :], 1.0, 0.0
    ).reshape(1, -1)
    places = my_index * groups + jnp.arange(groups, dtype=jnp.int32)
    arriving = jnp.sum(
        jnp.where(
            handover[None, :] == places[:, None],
            jnp.arange(total_groups, dtype=jnp.int32)[None, :],
            0,
        ),
        axis=1,
    )
    sources = arriving // groups

    send = pl.pallas_call(
        functools.partial(first_round, scale_in, scale_out),
        out_shape=jax.ShapeDtypeStruct(slab, BF16),
        in_specs=[smem, vmem] + [anywhere] * 4,
        out_specs=vmem,
        scratch_shapes=[
            pltpu.VMEM((pool, width), BF16),
            pltpu.VMEM((pool, width), BF16),
            pltpu.VMEM((width, hidden), F32),
            pltpu.VMEM((width, hidden), F32),
            pltpu.VMEM((hidden, width), F32),
            pltpu.VMEM((hidden, width), F32),
            pltpu.VMEM((batch, width), BF16),
            pltpu.SemaphoreType.DMA((4,)),
        ],
        compiler_params=pltpu.CompilerParams(vmem_limit_bytes=VMEM_LIMIT),
        cost_estimate=pl.CostEstimate(
            flops=STEPS * 18 * batch * width * hidden, bytes_accessed=20 << 20, transcendentals=0
        ),
        name="first_round",
    )(chosen, row_picks, pool_inputs, pool_targets, weight_in, weight_out)

    rows_shape = (STEPS, batch, width)
    landed, rows, goals, prediction = pl.pallas_call(
        functools.partial(hand_over, owners, scale_in, scale_out),
        out_shape=[
            jax.ShapeDtypeStruct(slab, BF16),
            jax.ShapeDtypeStruct(rows_shape, BF16),
            jax.ShapeDtypeStruct(rows_shape, BF16),
            jax.ShapeDtypeStruct((16, piece), F32),
        ],
        in_specs=[anywhere, vmem, anywhere, anywhere, vmem, vmem],
        out_specs=[anywhere, anywhere, anywhere, vmem],
        scratch_shapes=[
            pltpu.VMEM(slab, BF16),
            pltpu.VMEM((pool, width), BF16),
            pltpu.VMEM((pool, width), BF16),
            pltpu.VMEM(rows_shape, BF16),
            pltpu.VMEM(rows_shape, BF16),
            pltpu.VMEM((per_owner * owners, width), F32),
            pltpu.VMEM((owners, 16, piece), BF16),
            pltpu.SemaphoreType.DMA((owners,)),
            pltpu.SemaphoreType.DMA((owners,)),
            pltpu.SemaphoreType.DMA((owners,)),
            pltpu.SemaphoreType.DMA((owners,)),
            pltpu.SemaphoreType.DMA((bits,)),
            pltpu.SemaphoreType.DMA((bits,)),
            pltpu.SemaphoreType.DMA((4,)),
            pltpu.SemaphoreType.DMA((2,)),
        ]
        + [pltpu.VMEM((owners >> (bit + 1), 2, 16, piece), BF16) for bit in range(bits)]
        + [pltpu.VMEM((owners >> (bit + 1), 16, piece), BF16) for bit in range(bits)],
        compiler_params=pltpu.CompilerParams(
            vmem_limit_bytes=VMEM_LIMIT, collective_id=0, has_side_effects=True
        ),
        cost_estimate=pl.CostEstimate(
            flops=STEPS * 8 * batch * width * hidden, bytes_accessed=40 << 20, transcendentals=0
        ),
        name="hand_over",
    )(send, row_picks, pool_inputs, pool_targets, evals, valid)

    trained_in, trained_out = pl.pallas_call(
        functools.partial(second_round, scale_in, scale_out),
        out_shape=[jax.ShapeDtypeStruct((width, hidden), F32)] * 2,
        in_specs=[smem, anywhere, anywhere, anywhere],
        out_specs=[anywhere, anywhere],
        scratch_shapes=[
            pltpu.VMEM((groups, 2 * GROUP, width), BF16),
            pltpu.VMEM((hidden, width), F32),
            pltpu.VMEM((hidden, width), F32),
            pltpu.VMEM(rows_shape, BF16),
            pltpu.VMEM(rows_shape, BF16),
            pltpu.VMEM((width, hidden), F32),
            pltpu.VMEM((width, hidden), F32),
            pltpu.SemaphoreType.DMA((groups,)),
            pltpu.SemaphoreType.DMA((STEPS,)),
            pltpu.SemaphoreType.DMA((STEPS,)),
            pltpu.SemaphoreType.DMA((2 * (width // CHUNK),)),
        ],
        compiler_params=pltpu.CompilerParams(vmem_limit_bytes=VMEM_LIMIT),
        cost_estimate=pl.CostEstimate(
            flops=STEPS * 10 * batch * width * hidden, bytes_accessed=28 << 20, transcendentals=0
        ),
        name="second_round",
    )(sources, landed, rows, goals)

    prediction = (
        prediction.reshape(pieces, per_owner, piece)
        .transpose(1, 0, 2)
        .reshape(per_owner, width)
    )
    return (trained_in, trained_out, prediction)


def solution(mesh):
    in_specs = (
        P("sub", None),
        P("sub", None),
        P(None, "sub"),
        P(None, "sub"),
        P(None, "sub"),
        P("sub", None),
        P(),
    )
    out_specs = (P(None, "sub"), P(None, "sub"), P("sub", None))
    return jax.shard_map(
        per_device, mesh=mesh, in_specs=in_specs, out_specs=out_specs, check_vma=False
    )
```

```python
import functools
import math

import jax
import jax.numpy as jnp
from jax import lax
from jax.experimental import pallas as pl
from jax.experimental.pallas import tpu as pltpu
from jax.sharding import PartitionSpec as P

GROUP = 8
STEPS = 4
CHUNK = 1024
VMEM_LIMIT = 58 * 1024 * 1024
MESH_IDS = pl.DeviceIdType.MESH

tanh_coef = 0.7978845608028654
cubic_coef = 0.044715
step_rate = 0.5
F32 = jnp.float32
BF16 = jnp.bfloat16


def gelu_value(inputs):
    inner_term = tanh_coef * (inputs + cubic_coef * inputs * inputs * inputs)
    return 0.5 * inputs * (1.0 + jnp.tanh(inner_term))


def gelu_parts(inputs):
    tanh_part = jnp.tanh(tanh_coef * (inputs + cubic_coef * inputs * inputs * inputs))
    values = 0.5 * inputs * (1.0 + tanh_part)
    slopes = 0.5 * (1.0 + tanh_part) + 0.5 * inputs * (1.0 - tanh_part * tanh_part) * tanh_coef * (
        1.0 + 3.0 * cubic_coef * inputs * inputs
    )
    return (values, slopes)


def dot_nn(left, right):
    return jnp.dot(left, right, preferred_element_type=F32)


def dot_nt(left, right):
    return lax.dot_general(left, right, (((1,), (1,)), ((), ())), preferred_element_type=F32)


def chunks_of(width):
    return [pl.ds(first, CHUNK) for first in range(0, width, CHUNK)]


def one_hot(picks_t, turn, pool):
    turns = lax.broadcasted_iota(jnp.int32, picks_t.shape, 1)
    picks = jnp.sum(jnp.where(turns == turn, picks_t, 0.0), axis=1, keepdims=True)
    places = lax.broadcasted_iota(jnp.int32, (picks.shape[0], pool), 1).astype(F32)
    return jnp.where(places == picks, 1.0, 0.0).astype(BF16)


def train_step(in_t, out_t, rows_at, goals_at, scale_in, scale_out):
    width = in_t.shape[1]
    before = None
    for part in chunks_of(width):
        term = dot_nt(rows_at(part, True), in_t[:, part].astype(BF16))
        before = term if before is None else before + term
    values, slopes = gelu_parts(before * scale_in)
    activity = (values * scale_out).astype(BF16)
    activity_t = (values * (step_rate * scale_out)).T.astype(BF16)
    back = None
    for part in chunks_of(width):
        master = out_t[:, part]
        half = master.astype(BF16)
        errors = (dot_nn(activity, half) - goals_at(part)).astype(BF16)
        term = dot_nt(errors, half)
        back = term if back is None else back + term
        out_t[:, part] = master - dot_nn(activity_t, errors)
    backward_t = (back * (scale_out * scale_in * step_rate) * slopes).T.astype(BF16)
    for part in chunks_of(width):
        in_t[:, part] = in_t[:, part] - dot_nn(backward_t, rows_at(part, False))


def first_round(
    scale_in, scale_out,
    chosen, picks, pool_in, pool_out, weight_in, weight_out,
    send,
    inputs, targets, start_in, start_out, in_t, out_t, rows, load_sem,
):
    width, pool = weight_in.shape[0], pool_in.shape[0]
    loads = [
        pltpu.make_async_copy(source, target, load_sem.at[k])
        for k, (source, target) in enumerate(
            [(weight_in, start_in), (weight_out, start_out), (pool_in, inputs), (pool_out, targets)]
        )
    ]
    for load in loads:
        load.start()
    picks_t = picks[...].astype(F32).T
    loads[0].wait()
    for part in chunks_of(width):
        in_t[:, part] = start_in[part, :].T
    loads[1].wait()
    for part in chunks_of(width):
        out_t[:, part] = start_out[part, :].T
    loads[2].wait()
    loads[3].wait()

    @pl.loop(0, STEPS)
    def _(turn):
        select = one_hot(picks_t, turn, pool)

        def rows_at(part, fresh):
            if fresh:
                rows[:, part] = dot_nn(select, inputs[:, part]).astype(BF16)
            return rows[:, part]

        def goals_at(part):
            return dot_nn(select, targets[:, part])

        train_step(in_t, out_t, rows_at, goals_at, scale_in, scale_out)

    @pl.loop(0, send.shape[0])
    def _(owner):
        place = pl.ds(pl.multiple_of(chosen[owner] * GROUP, GROUP), GROUP)
        send[owner] = jnp.concatenate([in_t[place, :], out_t[place, :]], axis=0).astype(BF16)


def hand_over(
    owners, scale_in, scale_out,
    send, picks, pool_in, pool_out, evals_0, evals_1, evals_2, evals_3, valid,
    landed, rows_out, goals_out, prediction,
    sent, inputs, targets, rows, goals, all_evals, quad, gathered,
    send_sem, recv_sem, eval_send, eval_recv, share_send, share_recv, local_sem, out_sem,
    *sums,
):
    me = lax.axis_index("sub")
    bits = owners.bit_length() - 1
    kept, added = sums[:bits], sums[bits:]
    barrier = pltpu.get_barrier_semaphore()

    def other(turn):
        return lax.rem(me + turn, owners)

    @pl.loop(1, owners)
    def _(turn):
        pl.semaphore_signal(barrier, inc=1, device_id=(other(turn),), device_id_type=MESH_IDS)

    sent_copy = pltpu.make_async_copy(send, sent, local_sem.at[0])
    own_copy = pltpu.make_async_copy(send.at[me], landed.at[me], local_sem.at[1])
    inputs_copy = pltpu.make_async_copy(pool_in, inputs, local_sem.at[2])
    targets_copy = pltpu.make_async_copy(pool_out, targets, local_sem.at[3])
    sent_copy.start()
    own_copy.start()
    inputs_copy.start()
    targets_copy.start()
    quarter = owners // 4
    high, low = me // quarter, lax.rem(me, quarter)
    for hop, slab in enumerate((evals_0, evals_1, evals_2, evals_3)):
        quad[lax.rem(high - hop + 4, 4)] = slab[...]
        gathered[low, lax.rem(high - hop + 4, 4)] = slab[...]
    pl.semaphore_wait(barrier, owners - 1)

    def spreading(turn, arriving):
        low_peer = lax.rem(low + turn, quarter)
        return pltpu.make_async_remote_copy(
            src_ref=quad, dst_ref=gathered.at[low],
            send_sem=eval_send.at[low_peer], recv_sem=eval_recv.at[low_peer if arriving else low],
            device_id=(high * quarter + low_peer,), device_id_type=MESH_IDS,
        )

    def moving(peer, slot):
        return pltpu.make_async_remote_copy(
            src_ref=send.at[peer], dst_ref=landed.at[me],
            send_sem=send_sem.at[peer], recv_sem=recv_sem.at[slot],
            device_id=(peer,), device_id_type=MESH_IDS,
        )

    def summing(bit):
        mine = lax.rem(me // (1 << bit), 2)
        peer = me + (1 - 2 * mine) * (1 << bit)
        return mine, pltpu.make_async_remote_copy(
            src_ref=kept[bit].at[:, 1 - mine], dst_ref=added[bit],
            send_sem=share_send.at[bit], recv_sem=share_recv.at[bit],
            device_id=(peer,), device_id_type=MESH_IDS,
        )

    @pl.loop(1, quarter)
    def _(turn):
        spreading(turn, False).start()

    def move_some(first, last):
        @pl.loop(first, last)
        def _(step):
            low_peer = lax.rem(low + step + 1, quarter)
            for hop in (2, 1, 3):
                peer = lax.rem(high + hop, 4) * quarter + low_peer
                moving(peer, me).start()

            @pl.when(step < quarter - 1)
            def _():
                moving(high * quarter + low_peer, me).start()

    cuts = [quarter * (k + 1) // (bits + 1) for k in range(bits)] + [quarter]
    cuts[0] = max(cuts[0], 2)
    cuts = [0] + [max(cuts[0], cut) for cut in cuts]
    move_some(cuts[0], cuts[1])

    sent_copy.wait()
    per_owner = all_evals.shape[0] // owners
    slots = owners * 2 * GROUP
    width = sent.shape[2]
    pieces, piece = 16 // per_owner, width * per_owner // 16
    together = 8 // per_owner

    @pl.loop(1, quarter)
    def _(turn):
        spreading(turn, False).wait_send()
        spreading(turn, True).wait_recv()

    @pl.loop(0, owners // together)
    def _(block):
        first = block * together
        slabs = [
            gathered[lax.rem(first, quarter) + k, first // quarter].astype(F32)
            for k in range(together)
        ]
        for k in range(pieces):
            all_evals[pl.ds(pl.multiple_of(block * 8, 8), 8), pl.ds(k * piece, piece)] = (
                jnp.concatenate([slab[k * per_owner : (k + 1) * per_owner] for slab in slabs], axis=0)
            )

    before = dot_nt(all_evals[...].astype(BF16), sent[...].reshape(slots, width)) * scale_in
    acts = (pltpu.roll(gelu_value(before), GROUP, 1) * valid[...]).astype(BF16)
    partial = all_evals
    for part in chunks_of(width):
        partial[:, part] = dot_nn(acts, sent[:, :, part].reshape(slots, CHUNK)) * scale_out

    @pl.loop(0, owners // together)
    def _(block):
        tile = partial[pl.ds(pl.multiple_of(block * 8, 8), 8), :]
        for k in range(together):
            mine = tile[k * per_owner : (k + 1) * per_owner]
            kept[0][block * (together // 2) + k // 2, k % 2] = jnp.concatenate(
                [mine[:, j * piece : (j + 1) * piece] for j in range(pieces)], axis=0
            ).astype(kept[0].dtype)

    inputs_copy.wait()
    targets_copy.wait()
    pool = inputs.shape[0]
    picks_t = picks[...].astype(F32).T

    for bit in range(bits):
        mine, share = summing(bit)
        share.start()
        move_some(cuts[bit + 1], cuts[bit + 2])
        if bit < STEPS:
            select = one_hot(picks_t, STEPS + bit, pool)

            @pl.loop(0, width // CHUNK)
            def _(k):
                part = pl.ds(pl.multiple_of(k * CHUNK, CHUNK), CHUNK)
                rows[bit, :, part] = dot_nn(select, inputs[:, part]).astype(BF16)
                goals[bit, :, part] = dot_nn(select, targets[:, part]).astype(BF16)

        if bit == STEPS - 1:
            pltpu.make_async_copy(rows, rows_out, out_sem.at[0]).start()
            pltpu.make_async_copy(goals, goals_out, out_sem.at[1]).start()
        share.wait()
        if bit < bits - 1:
            @pl.loop(0, owners >> (bit + 2))
            def _(pair):
                for k in range(2):
                    slot = 2 * pair + k
                    kept[bit + 1][pair, k] = (
                        kept[bit][slot, mine].astype(F32) + added[bit][slot].astype(F32)
                    ).astype(kept[bit + 1].dtype)
        else:
            prediction[...] = kept[bit][0, mine] + added[bit][0]

    pltpu.make_async_copy(rows, rows_out, out_sem.at[0]).wait()
    pltpu.make_async_copy(goals, goals_out, out_sem.at[1]).wait()
    own_copy.wait()

    @pl.loop(1, owners)
    def _(turn):
        moving(other(turn), me).wait_send()
        moving(other(turn), other(turn)).wait_recv()


def second_round(
    scale_in, scale_out, sources, landed, rows_in, goals_in, trained_in, trained_out,
    handed, in_t, out_t, rows, goals, done_in, done_out, handed_sem, rows_sem, goals_sem, done_sem,
):
    groups = handed.shape[0]

    def fetch(slot):
        return pltpu.make_async_copy(landed.at[sources[slot]], handed.at[slot], handed_sem.at[slot])

    def rows_copy(turn):
        return pltpu.make_async_copy(rows_in.at[turn], rows.at[turn], rows_sem.at[turn])

    def goals_copy(turn):
        return pltpu.make_async_copy(goals_in.at[turn], goals.at[turn], goals_sem.at[turn])

    @pl.loop(0, groups)
    def _(slot):
        fetch(slot).start()

    @pl.loop(0, STEPS)
    def _(turn):
        rows_copy(turn).start()
        goals_copy(turn).start()

    @pl.loop(0, groups)
    def _(slot):
        fetch(slot).wait()
        slab = handed[slot].astype(F32)
        place = pl.ds(pl.multiple_of(slot * GROUP, GROUP), GROUP)
        in_t[place, :] = slab[:GROUP]
        out_t[place, :] = slab[GROUP:]

    @pl.loop(0, STEPS)
    def _(turn):
        rows_copy(turn).wait()
        goals_copy(turn).wait()
        train_step(
            in_t, out_t,
            lambda part, fresh: rows[turn, :, part],
            lambda part: goals[turn, :, part].astype(F32),
            scale_in, scale_out,
        )

    stores = []
    for k, part in enumerate(chunks_of(in_t.shape[1])):
        for side, (master, done, trained) in enumerate(
            [(in_t, done_in, trained_in), (out_t, done_out, trained_out)]
        ):
            done[part, :] = master[:, part].T
            stores.append(
                pltpu.make_async_copy(done.at[part, :], trained.at[part, :], done_sem.at[2 * k + side])
            )
            stores[-1].start()
    for store in stores:
        store.wait()


def per_device(pool_inputs, pool_targets, row_picks, weight_in, weight_out, eval_inputs, handover):
    owners = lax.axis_size("sub")
    my_index = lax.axis_index("sub")
    width, hidden = weight_in.shape
    pool = pool_inputs.shape[0]
    batch = row_picks.shape[1]
    per_owner = eval_inputs.shape[0]
    groups = hidden // GROUP
    total_groups = groups * owners
    scale_in = 1.0 / math.sqrt(width)
    scale_out = 1.0 / math.sqrt(hidden * owners)
    vmem = pl.BlockSpec(memory_space=pltpu.VMEM)
    smem = pl.BlockSpec(memory_space=pltpu.SMEM)
    anywhere = pl.BlockSpec(memory_space=pl.ANY)
    slab = (owners, 2 * GROUP, width)
    bits = owners.bit_length() - 1

    pieces = 16 // per_owner
    piece = width // pieces
    evals = eval_inputs.reshape(per_owner, pieces, piece).transpose(1, 0, 2).reshape(16, piece)
    quarter = owners // 4
    evals = [evals] + [
        lax.ppermute(
            evals, "sub",
            [(d, ((d // quarter + hop) % 4) * quarter + d % quarter) for d in range(owners)],
        )
        for hop in (1, 2, 3)
    ]

    targets = lax.dynamic_slice_in_dim(handover, my_index * groups, groups, 0) // groups
    matches = targets[None, :] == jnp.arange(owners, dtype=jnp.int32)[:, None]
    chosen = jnp.sum(jnp.where(matches, jnp.arange(groups, dtype=jnp.int32)[None, :], 0), axis=1)
    has_group = jnp.any(matches, axis=1)
    valid = jnp.where(
        has_group[:, None] & (jnp.arange(2 * GROUP) >= GROUP)[None, :], 1.0, 0.0
    ).reshape(1, -1)
    places = my_index * groups + jnp.arange(groups, dtype=jnp.int32)
    arriving = jnp.sum(
        jnp.where(
            handover[None, :] == places[:, None],
            jnp.arange(total_groups, dtype=jnp.int32)[None, :],
            0,
        ),
        axis=1,
    )
    sources = arriving // groups

    send = pl.pallas_call(
        functools.partial(first_round, scale_in, scale_out),
        out_shape=jax.ShapeDtypeStruct(slab, BF16),
        in_specs=[smem, vmem] + [anywhere] * 4,
        out_specs=vmem,
        scratch_shapes=[
            pltpu.VMEM((pool, width), BF16),
            pltpu.VMEM((pool, width), BF16),
            pltpu.VMEM((width, hidden), F32),
            pltpu.VMEM((width, hidden), F32),
            pltpu.VMEM((hidden, width), F32),
            pltpu.VMEM((hidden, width), F32),
            pltpu.VMEM((batch, width), BF16),
            pltpu.SemaphoreType.DMA((4,)),
        ],
        compiler_params=pltpu.CompilerParams(vmem_limit_bytes=VMEM_LIMIT),
        cost_estimate=pl.CostEstimate(
            flops=STEPS * 18 * batch * width * hidden, bytes_accessed=20 << 20, transcendentals=0
        ),
        name="first_round",
    )(chosen, row_picks, pool_inputs, pool_targets, weight_in, weight_out)

    rows_shape = (STEPS, batch, width)
    landed, rows, goals, prediction = pl.pallas_call(
        functools.partial(hand_over, owners, scale_in, scale_out),
        out_shape=[
            jax.ShapeDtypeStruct(slab, BF16),
            jax.ShapeDtypeStruct(rows_shape, BF16),
            jax.ShapeDtypeStruct(rows_shape, BF16),
            jax.ShapeDtypeStruct((16, piece), F32),
        ],
        in_specs=[anywhere, vmem, anywhere, anywhere] + [vmem] * 5,
        out_specs=[anywhere, anywhere, anywhere, vmem],
        scratch_shapes=[
            pltpu.VMEM(slab, BF16),
            pltpu.VMEM((pool, width), BF16),
            pltpu.VMEM((pool, width), BF16),
            pltpu.VMEM(rows_shape, BF16),
            pltpu.VMEM(rows_shape, BF16),
            pltpu.VMEM((per_owner * owners, width), F32),
            pltpu.VMEM((4, 16, piece), BF16),
            pltpu.VMEM((owners // 4, 4, 16, piece), BF16),
            pltpu.SemaphoreType.DMA((owners,)),
            pltpu.SemaphoreType.DMA((owners,)),
            pltpu.SemaphoreType.DMA((owners // 4,)),
            pltpu.SemaphoreType.DMA((owners // 4,)),
            pltpu.SemaphoreType.DMA((bits,)),
            pltpu.SemaphoreType.DMA((bits,)),
            pltpu.SemaphoreType.DMA((4,)),
            pltpu.SemaphoreType.DMA((2,)),
        ]
        + [pltpu.VMEM((owners >> (bit + 1), 2, 16, piece), F32 if bit > 1 else BF16) for bit in range(bits)]
        + [pltpu.VMEM((owners >> (bit + 1), 16, piece), F32 if bit > 1 else BF16) for bit in range(bits)],
        compiler_params=pltpu.CompilerParams(
            vmem_limit_bytes=VMEM_LIMIT, collective_id=0, has_side_effects=True
        ),
        cost_estimate=pl.CostEstimate(
            flops=STEPS * 8 * batch * width * hidden, bytes_accessed=40 << 20, transcendentals=0
        ),
        name="hand_over",
    )(send, row_picks, pool_inputs, pool_targets, *evals, valid)

    trained_in, trained_out = pl.pallas_call(
        functools.partial(second_round, scale_in, scale_out),
        out_shape=[jax.ShapeDtypeStruct((width, hidden), F32)] * 2,
        in_specs=[smem, anywhere, anywhere, anywhere],
        out_specs=[anywhere, anywhere],
        scratch_shapes=[
            pltpu.VMEM((groups, 2 * GROUP, width), BF16),
            pltpu.VMEM((hidden, width), F32),
            pltpu.VMEM((hidden, width), F32),
            pltpu.VMEM(rows_shape, BF16),
            pltpu.VMEM(rows_shape, BF16),
            pltpu.VMEM((width, hidden), F32),
            pltpu.VMEM((width, hidden), F32),
            pltpu.SemaphoreType.DMA((groups,)),
            pltpu.SemaphoreType.DMA((STEPS,)),
            pltpu.SemaphoreType.DMA((STEPS,)),
            pltpu.SemaphoreType.DMA((2 * (width // CHUNK),)),
        ],
        compiler_params=pltpu.CompilerParams(vmem_limit_bytes=VMEM_LIMIT),
        cost_estimate=pl.CostEstimate(
            flops=STEPS * 10 * batch * width * hidden, bytes_accessed=28 << 20, transcendentals=0
        ),
        name="second_round",
    )(sources, landed, rows, goals)

    prediction = (
        prediction.reshape(pieces, per_owner, piece)
        .transpose(1, 0, 2)
        .reshape(per_owner, width)
    )
    return (trained_in, trained_out, prediction)


def solution(mesh):
    in_specs = (
        P("sub", None),
        P("sub", None),
        P(None, "sub"),
        P(None, "sub"),
        P(None, "sub"),
        P("sub", None),
        P(),
    )
    out_specs = (P(None, "sub"), P(None, "sub"), P("sub", None))
    return jax.shard_map(
        per_device, mesh=mesh, in_specs=in_specs, out_specs=out_specs, check_vma=False
    )
```
